32 devices in a mesh: seq: 8 (over z, y), head: 4 (over x, core).
Axes of the slice: x: 2, y: 2, z: 4, core: 2. Of those that a mesh axis runs over, the one named last changes fastest.
Arguments:
- query_rows: bfloat16 [2, 2048, 1024], P(None, 'seq', 'head'), may hold values from -70 to 70
- key_rows: bfloat16 [2, 2048, 1024], P(None, 'seq', 'head'), may hold values from -4.5 to 4.5
- value_rows: bfloat16 [2, 2048, 1024], P(None, 'seq', 'head'), may hold values from -6 to 6
- first_fast: float32 [4, 256, 512], P('head'), may hold values from -0.375 to 0.375
- third_fast: float32 [4, 256, 512], P('head'), may hold values from -0.375 to 0.375
- second_fast: float32 [4, 512, 256], P('head'), may hold values from -0.25 to 0.25
- out_proj: bfloat16 [1024, 1024], P('head'), may hold values from -0.1875 to 0.1875
- teacher: bfloat16 [2, 2048, 1024], P(None, 'seq'), may hold values from -31 to 31
Outputs:
- student: bfloat16 [2, 2048, 1024], P(None, 'seq', 'head')
- out_grad: float32 [1024, 1024], P('head')
- new_first: float32 [4, 256, 512], P('head')
- new_third: float32 [4, 256, 512], P('head')
- new_second: float32 [4, 512, 256], P('head')
- distill_loss: float32 [], replicated
The draws below stay inside these ranges and needn't reach their ends.
All inputs are finite; a program needn't handle non-finite values.
Results may differ from the reference program's by a relative error of at most 0.012.
Values may be sent and summed in bfloat16 or wider, within the bound.
No kernel may reach another device: no remote copies, remote signals or barrier semaphores. Data moves between devices by JAX's collectives and lax.ppermute only.
A program may use at most 64 MiB of HBM per device.

```python
import math
import jax
import jax.numpy as jnp
from jax import lax

D = 1024
HEADS = 4
FF = 512
WINDOW = 256
NS_STEPS = 5
GROUPS = 2
HD = 256
GROUP = 2048


def draw_pairs(key):
    base_key = jax.random.fold_in(key, 711)
    key_part = jax.random.fold_in(base_key, 1)
    query_part = jax.random.fold_in(base_key, 2)
    total_rows = GROUPS * GROUP
    col_count = HEADS * HD
    keys_all = jnp.clip(jax.random.normal(key_part, (total_rows, col_count), jnp.float32), -4.5, 4.5)
    queries = jnp.clip(jax.random.normal(query_part, (total_rows, col_count), jnp.float32), -4.5, 4.5)
    return (queries.reshape(GROUPS, GROUP, col_count), keys_all.reshape(GROUPS, GROUP, col_count))


def draw_query_rows(key, part):
    return draw_pairs(key)[0].astype(jnp.bfloat16)


def draw_key_rows(key, part):
    return draw_pairs(key)[1].astype(jnp.bfloat16)


def draw_teacher(key, part):
    total_rows = GROUPS * GROUP
    noise = jnp.clip(jax.random.normal(jax.random.fold_in(key, 913), (total_rows, D), jnp.float32), -5.0, 5.0)
    ramp = 0.5 * jnp.exp(math.log(4.0) * jnp.arange(total_rows, dtype=jnp.float32) / (total_rows - 1))
    return (noise * ramp[:, None]).reshape(GROUPS, GROUP, D).astype(jnp.bfloat16)


def shard_levels(stream_key, extent, split, low, largest):
    def one(dim, parts):
        draws = jax.random.uniform(jax.random.fold_in(jax.random.fold_in(stream_key, 6), dim), (parts,), jnp.float32, low / len(split), largest / len(split))
        return jnp.repeat(jnp.exp(draws), extent[dim] // parts).reshape((-1,) + (1,) * (len(extent) - dim - 1))

    loudness = one(*split[0])
    for cut in split[1:]:
        loudness = loudness * one(*cut)
    return loudness


def centred(own_key, shape, spread, reach, split=(), kind=jnp.bfloat16):
    level = shard_levels(own_key, shape, split, -0.22, 0.18) if split else 1.0
    array = jax.random.normal(own_key, shape, jnp.float32) * spread * level
    return jnp.minimum(jnp.maximum(array, -reach), reach).astype(kind)


def setup_inputs(seed: int = 0) -> dict:
    streams_of = jax.random.split(jax.random.key(seed), 9)
    return {
        "query_rows": draw_query_rows(jax.random.fold_in(streams_of[8], 71), 0),
        "key_rows": draw_key_rows(jax.random.fold_in(streams_of[8], 71), 0),
        "value_rows": centred(streams_of[2], (GROUPS, GROUP, D), 1.0, 6.0, ((1, 8), (2, 4))),
        "first_fast": centred(streams_of[3], (HEADS, HD, FF), HD ** -0.5, 0.375, ((0, 4),), jnp.float32),
        "third_fast": centred(streams_of[4], (HEADS, HD, FF), HD ** -0.5, 0.375, ((0, 4),), jnp.float32),
        "second_fast": centred(streams_of[5], (HEADS, FF, HD), FF ** -0.5, 0.25, ((0, 4),), jnp.float32),
        "out_proj": centred(streams_of[6], (D, D), D ** -0.5, 0.1875, ((0, 4),)),
        "teacher": draw_teacher(jax.random.fold_in(streams_of[8], 71), 0),
    }


PRECISE = lax.Precision.HIGHEST
SCHULZ_COEFFS = (3.4445, -4.775, 2.0315)
LEARN_RATE = 0.5
EPSILON = 1e-06

def orthogonalize(matrix):
    current = matrix / (jnp.sqrt(jnp.sum(matrix * matrix)) + EPSILON)
    for sweep in range(NS_STEPS):
        gram_mat = jnp.dot(current, current.T, precision=PRECISE)
        poly_mat = SCHULZ_COEFFS[1] * gram_mat + SCHULZ_COEFFS[2] * jnp.dot(gram_mat, gram_mat, precision=PRECISE)
        current = SCHULZ_COEFFS[0] * current + jnp.dot(poly_mat, current, precision=PRECISE)
    return current

def fast_forward(w_one, w_three, w_two, inputs):
    gate_act = jnp.dot(inputs, w_one, precision=PRECISE)
    up_act = jnp.dot(inputs, w_three, precision=PRECISE)
    hidden = jax.nn.silu(gate_act) * up_act
    return (jnp.dot(hidden, w_two, precision=PRECISE), gate_act, up_act, hidden)

def fast_gradients(w_one, w_three, w_two, inputs, targets):
    unused, gate_act, up_act, hidden = fast_forward(w_one, w_three, w_two, inputs)
    grad_two = -jnp.dot(hidden.T, targets, precision=PRECISE)
    d_hidden = -jnp.dot(targets, w_two.T, precision=PRECISE)
    sigmoid_gate = jax.nn.sigmoid(gate_act)
    d_gate = d_hidden * up_act * sigmoid_gate * (1.0 + gate_act * (1.0 - sigmoid_gate))
    d_up = d_hidden * gate_act * sigmoid_gate
    grad_one = jnp.dot(inputs.T, d_gate, precision=PRECISE)
    grad_three = jnp.dot(inputs.T, d_up, precision=PRECISE)
    return (grad_one, grad_three, grad_two)

def fast_update(w_one, w_three, w_two, grads):
    return (w_one - LEARN_RATE * orthogonalize(grads[0]), w_three - LEARN_RATE * orthogonalize(grads[1]), w_two - LEARN_RATE * orthogonalize(grads[2].T).T)

def rms_scale(values):
    return values * lax.rsqrt(lax.optimization_barrier(jnp.mean(values * values, axis=-1, keepdims=True)) + EPSILON)

def window_attention(queries, keys, values):
    total_rows = queries.shape[0]
    blocks = total_rows // WINDOW
    pad_keys = jnp.concatenate([jnp.zeros((WINDOW, HD), keys.dtype), keys], axis=0)
    pad_values = jnp.concatenate([jnp.zeros((WINDOW, HD), values.dtype), values], axis=0)

    def one_block(block_idx):
        first_row = (block_idx * WINDOW).astype(jnp.int32)
        query_blk = lax.dynamic_slice_in_dim(queries, first_row, WINDOW, 0)
        key_blk = lax.dynamic_slice_in_dim(pad_keys, first_row, 2 * WINDOW, 0)
        value_blk = lax.dynamic_slice_in_dim(pad_values, first_row, 2 * WINDOW, 0)
        query_pos = first_row + jnp.arange(WINDOW, dtype=jnp.int32)
        key_pos = first_row - WINDOW + jnp.arange(2 * WINDOW, dtype=jnp.int32)
        scores = jnp.dot(query_blk, key_blk.T, preferred_element_type=jnp.float32) * (1.0 / math.sqrt(HD))
        spacing = query_pos[:, None] - key_pos[None, :]
        allowed = (spacing >= 0) & (spacing < WINDOW) & (key_pos[None, :] >= 0)
        masked = jnp.where(allowed, scores, -1e+30)
        top_score = lax.optimization_barrier(jnp.max(masked, axis=1, keepdims=True))
        expd = jnp.where(allowed, jnp.exp(masked - top_score), 0.0)
        weights = (expd / lax.optimization_barrier(jnp.sum(expd, axis=1, keepdims=True))).astype(jnp.bfloat16)
        return jnp.dot(weights, value_blk, preferred_element_type=jnp.float32)
    return lax.map(one_block, jnp.arange(blocks, dtype=jnp.int32)).reshape(total_rows, HD)

def reference(query_rows, key_rows, value_rows, first_fast, third_fast, second_fast, out_proj, teacher):
    total_rows = GROUPS * GROUP
    flat_q = query_rows.reshape(total_rows, D)
    flat_k = key_rows.reshape(total_rows, D)
    flat_v = value_rows.reshape(total_rows, D)
    mixed_heads = []
    firsts, thirds, seconds = ([], [], [])
    for head_idx in range(HEADS):
        lo_col = head_idx * HD
        hi_col = lo_col + HD
        attention = window_attention(flat_q[:, lo_col:hi_col], flat_k[:, lo_col:hi_col], flat_v[:, lo_col:hi_col]).reshape(GROUPS, GROUP, HD)
        w_one, w_three, w_two = (first_fast[head_idx], third_fast[head_idx], second_fast[head_idx])
        pieces = []
        for block_idx in range(GROUPS):
            q_float = query_rows[block_idx, :, lo_col:hi_col].astype(jnp.float32)
            k_float = key_rows[block_idx, :, lo_col:hi_col].astype(jnp.float32)
            v_float = value_rows[block_idx, :, lo_col:hi_col].astype(jnp.float32)
            fast_out = fast_forward(w_one, w_three, w_two, q_float)[0]
            pieces.append((attention[block_idx] + rms_scale(fast_out)).astype(jnp.bfloat16))
            grads = fast_gradients(w_one, w_three, w_two, k_float, v_float)
            w_one, w_three, w_two = fast_update(w_one, w_three, w_two, grads)
        mixed_heads.append(jnp.stack(pieces))
        firsts.append(w_one)
        thirds.append(w_three)
        seconds.append(w_two)
    mixed = jnp.concatenate(mixed_heads, axis=2).reshape(total_rows, D)
    summed = jnp.dot(mixed, out_proj, preferred_element_type=jnp.float32)
    student = summed.astype(jnp.bfloat16).reshape(GROUPS, GROUP, D)
    diff = summed - teacher.reshape(total_rows, D).astype(jnp.float32)
    resid = diff.astype(jnp.bfloat16)
    out_grad = jnp.dot(mixed.T, resid, preferred_element_type=jnp.float32) / math.sqrt(total_rows)
    distill_loss = jnp.sum(diff * diff) / (total_rows * D)
    return (student, out_grad, jnp.stack(firsts), jnp.stack(thirds), jnp.stack(seconds), distill_loss)
```

```python
import functools
import math

import jax
import jax.numpy as jnp
from jax import lax
from jax.experimental import pallas as pl
from jax.experimental.pallas import tpu as pltpu
from jax.sharding import PartitionSpec as P

WINDOW = 256
NS_STEPS = 5
SCHULZ_COEFFS = (3.4445, -4.775, 2.0315)
LEARN_RATE = 0.5
EPSILON = 1e-06
LANES = 128
LOSS_ROWS = 16
VMEM_BYTES = 40 * 1024 * 1024

F32 = jnp.float32
BF16 = jnp.bfloat16


def mm(a, b):
    return jnp.dot(a, b, preferred_element_type=F32)


def mm_nt(a, b):
    return lax.dot_general(a, b, (((1,), (1,)), ((), ())), preferred_element_type=F32)


def mm_tn(a, b):
    return lax.dot_general(a, b, (((0,), (0,)), ((), ())), preferred_element_type=F32)


def split(x):
    high = x.astype(BF16)
    return high, (x - high.astype(F32)).astype(BF16)


def token_gradients(weights, keys, values):
    w_one, w_three, w_two_t = weights
    gate = mm(keys, w_one)
    up = mm(keys, w_three)
    d_hidden = -mm(values, w_two_t)
    sig = jax.nn.sigmoid(gate)
    silu = gate * sig
    d_gate = d_hidden * up * sig * (1.0 + gate * (1.0 - sig))
    d_up = d_hidden * silu
    hidden = silu * up
    return (
        mm_tn(keys, d_gate.astype(BF16)),
        mm_tn(keys, d_up.astype(BF16)),
        -mm_tn(values, hidden.astype(BF16)),
    )


def orthogonalize(mats):
    a, b, c = SCHULZ_COEFFS
    centre = -b / (2.0 * c)
    rest = a - b * b / (4.0 * c)
    rows = mats[0].shape[0]
    shape = (rows, rows)
    diag = lax.broadcasted_iota(jnp.int32, shape, 0) == lax.broadcasted_iota(jnp.int32, shape, 1)
    xs = [m * (1.0 / (jnp.sqrt(jnp.sum(m * m)) + EPSILON)) for m in mats]
    for sweep in range(NS_STEPS):
        if sweep < 2:
            lows = [x.astype(BF16) for x in xs]
            grams = [mm_nt(x, x) for x in lows]
            halves = [g.astype(BF16) for g in grams]
            polys = [(b * g + c * mm(h, h)).astype(BF16) for g, h in zip(grams, halves)]
            xs = [a * x + mm(p, low) for x, p, low in zip(xs, polys, lows)]
        elif sweep == 2:
            pairs = [split(x) for x in xs]
            grams = [mm_nt(h, h) + mm_nt(h, l) + mm_nt(l, h) for h, l in pairs]
            gpairs = [split(g) for g in grams]
            polys = [
                b * g + c * (mm(h, h) + mm(h, l) + mm(l, h)) for g, (h, l) in zip(grams, gpairs)
            ]
            ppairs = [split(p) for p in polys]
            xs = [
                a * x + (mm(ph, h) + mm(ph, l) + mm(pl_, h))
                for x, (ph, pl_), (h, l) in zip(xs, ppairs, pairs)
            ]
        else:
            lows = [x.astype(BF16) for x in xs]
            grams = [mm_nt(x, x) for x in lows]
            moved = [jnp.where(diag, g - centre, g).astype(BF16) for g in grams]
            polys = [(c * mm(h, h)).astype(BF16) for h in moved]
            xs = [rest * x + mm(p, low) for x, p, low in zip(xs, polys, lows)]
    return xs


def normed_forward(weights, queries):
    w_one, w_three, w_two_t = [split(w) for w in weights]
    gate = mm(queries, w_one[0]) + mm(queries, w_one[1])
    up = mm(queries, w_three[0]) + mm(queries, w_three[1])
    hidden = (gate * jax.nn.sigmoid(gate) * up).astype(BF16)
    out = mm_nt(hidden, w_two_t[0]) + mm_nt(hidden, w_two_t[1])
    return out * lax.rsqrt(jnp.mean(out * out, axis=-1, keepdims=True) + EPSILON)


def window_attention(queries, own, behind, has_behind):
    tok, width = queries.shape
    head_dim = width
    scale = 1.0 / math.sqrt(head_dim)
    shape = (tok, tok)
    row = lax.broadcasted_iota(jnp.int32, shape, 0)
    col = lax.broadcasted_iota(jnp.int32, shape, 1)
    allow_own = (row >= col) & (row - col < WINDOW)
    allow_behind = (row + tok - col < WINDOW) & has_behind
    s_own = jnp.where(allow_own, mm_nt(queries, own[:, :width]) * scale, -1e30)
    s_behind = jnp.where(allow_behind, mm_nt(queries, behind[:, :width]) * scale, -1e30)
    top = jnp.maximum(
        jnp.max(s_own, axis=1, keepdims=True), jnp.max(s_behind, axis=1, keepdims=True)
    )
    e_own = jnp.where(allow_own, jnp.exp(s_own - top), 0.0)
    e_behind = jnp.where(allow_behind, jnp.exp(s_behind - top), 0.0)
    total = jnp.sum(e_own, axis=1, keepdims=True) + jnp.sum(e_behind, axis=1, keepdims=True)
    inv = 1.0 / total
    return mm((e_own * inv).astype(BF16), own[:, width:]) + mm(
        (e_behind * inv).astype(BF16), behind[:, width:]
    )


def call(kernel, outs, args, flops=0, scratch=()):
    vmem = pl.BlockSpec(memory_space=pltpu.VMEM)
    size = sum(math.prod(a.shape) * a.dtype.itemsize for a in list(args) + list(outs))
    return pl.pallas_call(
        kernel,
        out_shape=tuple(jax.ShapeDtypeStruct(o.shape, o.dtype) for o in outs),
        in_specs=[vmem] * len(args),
        out_specs=tuple([vmem] * len(outs)),
        scratch_shapes=list(scratch),
        compiler_params=pltpu.CompilerParams(vmem_limit_bytes=VMEM_BYTES),
        cost_estimate=pl.CostEstimate(flops=flops, bytes_accessed=size, transcendentals=0),
    )(*args)


def like(shape, dtype):
    return jax.ShapeDtypeStruct(shape, dtype)


def gradients(weights, runs, before):
    rows, hidden = weights[0].shape
    count = len(runs)

    def kernel(*refs):
        w = [r[...].astype(BF16) for r in refs[:3]]
        run_refs = refs[3 : 3 + count]
        prev = refs[3 + count : -3]
        sums = [p[...] for p in prev] if prev else None
        for run in run_refs:
            new = token_gradients(w, run[:, :rows], run[:, rows:])
            sums = list(new) if sums is None else [s + n for s, n in zip(sums, new)]
        for out, value in zip(refs[-3:], sums):
            out[...] = value

    tokens = sum(r.shape[0] for r in runs)
    args = list(weights) + list(runs) + (list(before) if before is not None else [])
    outs = [like((rows, hidden), F32)] * 3
    return call(kernel, outs, args, flops=12 * tokens * rows * hidden)


def update(weights, grads, last_runs, queries=None, attention=None, block=None):
    rows, hidden = weights[0].shape
    count = len(last_runs)
    mixes = queries is not None

    def kernel(*refs):
        w = [r[...] for r in refs[:3]]
        sums = [r[...] for r in refs[3:6]]
        run_refs = refs[6 : 6 + count]
        low = [x.astype(BF16) for x in w]
        for run in run_refs:
            new = token_gradients(low, run[:, :rows], run[:, rows:])
            sums = [s + n for s, n in zip(sums, new)]
        ortho = orthogonalize(sums)
        fresh = [x - LEARN_RATE * o for x, o in zip(w, ortho)]
        if mixes:
            q_ref, att_ref = refs[6 + count : 8 + count]
            outs = refs[8 + count :]
            for out, value in zip(outs, fresh):
                out[...] = value
            outs[3][...] = (att_ref[...] + normed_forward(fresh, q_ref[block])).astype(BF16)
        else:
            outs = refs[6 + count :]
            outs[0][0] = fresh[0]
            outs[1][0] = fresh[1]
            outs[2][0] = fresh[2].T

    args = list(weights) + list(grads) + list(last_runs)
    if mixes:
        args += [queries, attention]
        outs = [like((rows, hidden), F32)] * 3 + [like(queries.shape[1:], BF16)]
    else:
        outs = [like((1, rows, hidden), F32)] * 2 + [like((1, hidden, rows), F32)]
    flops = 3 * 5 * 2 * (2 * rows * rows * hidden + rows**3) * 2
    return call(kernel, outs, args, flops=flops)


def attend(queries, own, behind, block):
    def kernel(q_ref, own_ref, behind_ref, out_ref):
        has_behind = (lax.axis_index("seq") > 0) | (block > 0)
        out_ref[...] = window_attention(q_ref[block], own_ref[...], behind_ref[...], has_behind)

    tok, width = queries.shape[1:]
    return call(
        kernel, [like((tok, width), F32)], [queries, own, behind], flops=8 * tok * tok * width
    )[0]


def first_mix(queries, own, behind, weights):
    def kernel(q_ref, own_ref, behind_ref, one_ref, three_ref, two_ref, out_ref):
        has_behind = lax.axis_index("seq") > 0
        queries = q_ref[0]
        att = window_attention(queries, own_ref[...], behind_ref[...], has_behind)
        w = [one_ref[...], three_ref[...], two_ref[...]]
        out_ref[...] = (att + normed_forward(w, queries)).astype(BF16)

    tok, width = queries.shape[1:]
    return call(
        kernel,
        [like((tok, width), BF16)],
        [queries, own, behind] + list(weights),
        flops=20 * tok * tok * width,
    )[0]


def project(mixed_parts, proj_parts, teacher, block, students):
    count = len(mixed_parts)
    tok, width = mixed_parts[0].shape
    cols = teacher.shape[2]

    def kernel(*refs):
        mixed_refs, proj_refs = refs[:count], refs[count : 2 * count]
        teacher_ref = refs[2 * count]
        student_ref, resid_ref, loss_ref, low_ref = refs[2 * count + 1 :]
        summed = mm(mixed_refs[0][...], proj_refs[0][...])
        for m, p in zip(mixed_refs[1:], proj_refs[1:]):
            summed = summed + mm(m[...], p[...])
        low_ref[...] = summed.astype(BF16)
        start = pl.multiple_of(lax.axis_index("head") * width, width)
        student_ref[...] = low_ref[:, pl.ds(start, width)]
        diff = summed - teacher_ref[block].astype(F32)
        resid_ref[...] = diff.astype(BF16)
        loss_ref[...] = jnp.full((8, LANES), jnp.sum(diff * diff), F32)

    return call(
        kernel,
        [like((tok, width), BF16), like((tok, cols), BF16), like((8, LANES), F32)],
        list(mixed_parts) + list(proj_parts) + [teacher],
        flops=2 * tok * cols * width * count,
        scratch=[pltpu.VMEM((tok, cols), BF16)],
    )


def loss_tile(loss):
    high = loss.astype(BF16).astype(F32)
    row = lax.broadcasted_iota(jnp.int32, (LOSS_ROWS, LANES), 0)
    return jnp.where(row < LOSS_ROWS // 2, high, loss - high).astype(BF16)


def tile_loss(tile):
    return jnp.sum(tile.astype(F32)) * (1.0 / (LOSS_ROWS // 2 * LANES))


def outer_halves(mixed, resids, losses):
    count = len(mixed)
    width = mixed[0].shape[1]
    cols = resids[0].shape[1]
    half = cols // 2

    def kernel(*refs):
        mixed_refs, resid_refs = refs[:count], refs[count : 2 * count]
        loss_refs = refs[2 * count : 3 * count]
        keep_ref, send_ref, loss_ref = refs[3 * count :]
        mine = lax.rem(lax.axis_index("seq"), 2)
        keep_at = pl.multiple_of(mine * half, half)
        send_at = pl.multiple_of((1 - mine) * half, half)
        keep = send = None
        for m, r in zip(mixed_refs, resid_refs):
            one = mm_tn(m[...], r[:, pl.ds(send_at, half)])
            two = mm_tn(m[...], r[:, pl.ds(keep_at, half)])
            send = one if send is None else send + one
            keep = two if keep is None else keep + two
        keep_ref[...] = keep
        send_ref[:width, :] = send.astype(BF16)
        loss = sum(jnp.max(r[...]) for r in loss_refs)
        loss_ref[...] = jnp.full((8, LANES), loss, F32)
        tile = loss_tile(loss)
        for at in range(0, half, LANES):
            send_ref[width:, at : at + LANES] = tile

    return call(
        kernel,
        [like((width, half), F32), like((width + LOSS_ROWS, half), BF16), like((8, LANES), F32)],
        list(mixed) + list(resids) + list(losses),
        flops=2 * count * mixed[0].shape[0] * width * cols,
    )


def outer_chunks(keep, got, loss, line):
    width, half = keep.shape
    chunk = half // line

    def kernel(keep_ref, got_ref, loss_ref, own_ref, new_loss_ref, *rest):
        sends, full_ref = rest[:-1], rest[-1]
        place = lax.div(lax.axis_index("seq"), 2)
        full_ref[...] = keep_ref[...] + got_ref[:width, :].astype(F32)
        total = jnp.max(loss_ref[...]) + tile_loss(got_ref[width:, :LANES])
        new_loss_ref[...] = jnp.full((8, LANES), total, F32)
        tile = loss_tile(total)

        def part(index):
            return full_ref[:, pl.ds(pl.multiple_of(index * chunk, chunk), chunk)]

        own_ref[...] = part(place)
        for offset, send in enumerate(sends, start=1):
            send[:width, :] = part(place ^ offset).astype(BF16)
            for at in range(0, chunk, LANES):
                send[width:, at : at + LANES] = tile

    message = like((width + LOSS_ROWS, chunk), BF16)
    return call(
        kernel,
        [like((width, chunk), F32), like((8, LANES), F32)] + [message] * (line - 1),
        [keep, got, loss],
        scratch=[pltpu.VMEM((width, half), F32)],
    )


def outer_total(own, loss, gots, grad_scale, loss_scale):
    width, chunk = own.shape

    def kernel(own_ref, loss_ref, *rest):
        got_refs, out_ref, new_loss_ref = rest[:-2], rest[-2], rest[-1]
        total = own_ref[...]
        sq = jnp.max(loss_ref[...])
        for got in got_refs:
            total = total + got[:width, :].astype(F32)
            sq = sq + tile_loss(got[width:, :LANES])
        out_ref[...] = (total * grad_scale).astype(BF16)
        new_loss_ref[...] = jnp.full((8, LANES), sq * loss_scale, F32)

    return call(
        kernel, [like((width, chunk), BF16), like((8, LANES), F32)], [own, loss] + list(gots)
    )


def assemble(pieces, places, cols):
    width, chunk = pieces[0].shape
    count = len(pieces)

    def kernel(*refs):
        out_ref = refs[-1]
        me = lax.axis_index("seq")
        for ref, table in zip(refs[:count], places):
            index = sum(jnp.where(me == d, c, 0) for d, c in enumerate(table))
            out_ref[:, pl.ds(pl.multiple_of(index * chunk, chunk), chunk)] = ref[...].astype(F32)

    return call(kernel, [like((width, cols), F32)], list(pieces))[0]


def ring_order(size):
    return list(range(0, size, 2)) + list(range(size - 1 - size % 2, 0, -2))


def ring_steps(block, axis, split_last):
    size = lax.axis_size(axis)
    order = ring_order(size)
    ahead = [(order[i], order[(i + 1) % size]) for i in range(size)]
    back = [(b, a) for a, b in ahead]

    def source(distance):
        table = [0] * size
        for i, d in enumerate(order):
            table[d] = order[(i - distance) % size]
        return table

    steps = []
    up = down = block
    for step in range(1, size // 2 + 1):
        if 2 * step == size:
            if split_last:
                rows = block.shape[0] // 2
                steps.append(
                    [
                        (lax.ppermute(up[:rows], axis, ahead), source(step)),
                        (lax.ppermute(down[rows:], axis, back), source(step)),
                    ]
                )
            else:
                steps.append([(lax.ppermute(up, axis, ahead), source(step))])
        else:
            up = lax.ppermute(up, axis, ahead)
            down = lax.ppermute(down, axis, back)
            steps.append([(up, source(step)), (down, source(-step))])
    return steps


def partner(block, axis, bit):
    size = lax.axis_size(axis)
    return lax.ppermute(block, axis, [(i ^ bit, i) for i in range(size)])


def cube_gather(block, axis):
    parts = [block]
    bit = lax.axis_size(axis) // 2
    while bit:
        parts += [partner(p, axis, bit) for p in parts]
        bit //= 2
    return parts


def from_behind(block, axis):
    size = lax.axis_size(axis)
    return lax.ppermute(block, axis, [((i - 1) % size, i) for i in range(size)])


def local(query_rows, key_rows, value_rows, first_fast, third_fast, second_fast, out_proj, teacher):
    block_count, tok, head_dim = query_rows.shape
    seq = lax.axis_size("seq")
    cols = out_proj.shape[1]
    total_rows = block_count * tok * seq
    last = seq - 1
    pos = lax.axis_index("seq")
    gathers = seq <= 8
    kv = [jnp.concatenate([key_rows[c], value_rows[c]], axis=1) for c in range(block_count)]
    weights = (first_fast[0], third_fast[0], second_fast[0].T)

    proj_parts = cube_gather(out_proj, "head")
    behind = []
    for c in range(block_count):
        rim = kv[c] if c == 0 else jnp.where(pos == last, kv[c - 1], kv[c])
        behind.append(from_behind(rim, "seq"))

    students, resids, losses, mixed_rows = [], [], [], []
    mixed = first_mix(query_rows, kv[0], behind[0], weights)
    for c in range(block_count):
        mixed_rows.append(mixed)
        student, resid, loss = project(cube_gather(mixed, "head"), proj_parts, teacher, c, None)
        students.append(student)
        resids.append(resid)
        losses.append(loss)
        if gathers:
            steps = ring_steps(kv[c], "seq", True)
            runs = [[block for block, _ in step] for step in steps]
            grads = gradients(weights, [kv[c]] + (runs[0] if len(runs) > 1 else []), None)
            middle = [r for step in runs[1:-1] for r in step]
            if middle:
                grads = gradients(weights, middle, grads)
            final = runs[-1] if runs else []
        else:
            grads = lax.psum(gradients(weights, [kv[c]], None), "seq")
            final = []
        if c + 1 < block_count:
            attention = attend(query_rows, kv[c + 1], behind[c + 1], c + 1)
            *fresh, mixed = update(weights, grads, final, query_rows, attention, c + 1)
            weights = tuple(fresh)
        else:
            new_first, new_third, new_second = update(weights, grads, final)

    student = jnp.stack(students)
    grad_scale = 1.0 / math.sqrt(total_rows)
    loss_scale = 1.0 / (total_rows * cols)
    if seq >= 4 and seq & (seq - 1) == 0 and cols % (seq * LANES) == 0:
        line = seq // 2
        keep, send, loss = outer_halves(mixed_rows, resids, losses)
        own, loss, *sends = outer_chunks(keep, partner(send, "seq", 1), loss, line)
        gots = [partner(s, "seq", 2 * (m + 1)) for m, s in enumerate(sends)]
        piece, loss = outer_total(own, loss, gots, grad_scale, loss_scale)
        steps = ring_steps(piece, "seq", False)

        def place(d):
            return (d % 2) * line + d // 2

        pieces = [piece] + [p for step in steps for p, _ in step]
        tables = [list(range(seq))] + [t for step in steps for _, t in step]
        out_grad = assemble(pieces, [[place(d) for d in t] for t in tables], cols)
        distill_loss = loss[0, 0]
    else:
        term = sum(
            lax.dot_general(m, r, (((0,), (0,)), ((), ())), preferred_element_type=F32)
            for m, r in zip(mixed_rows, resids)
        )
        term, loss = lax.psum((term, sum(losses)), "seq")
        out_grad = term * grad_scale
        distill_loss = loss[0, 0] * loss_scale
    return (student, out_grad, new_first, new_third, new_second, distill_loss)


def solution(mesh):
    in_specs = (
        P(None, "seq", "head"),
        P(None, "seq", "head"),
        P(None, "seq", "head"),
        P("head", None, None),
        P("head", None, None),
        P("head", None, None),
        P("head", None),
        P(None, "seq", None),
    )
    out_specs = (
        P(None, "seq", "head"),
        P("head", None),
        P("head", None, None),
        P("head", None, None),
        P("head", None, None),
        P(),
    )
    return jax.shard_map(local, mesh=mesh, in_specs=in_specs, out_specs=out_specs, check_vma=False)
```

```python
import functools
import math

import jax
import jax.numpy as jnp
from jax import lax
from jax.experimental import pallas as pl
from jax.experimental.pallas import tpu as pltpu
from jax.sharding import PartitionSpec as P

WINDOW = 256
NS_STEPS = 5
SCHULZ_COEFFS = (3.4445, -4.775, 2.0315)
LEARN_RATE = 0.5
EPSILON = 1e-06
LANES = 128
LOSS_ROWS = 16
VMEM_BYTES = 40 * 1024 * 1024

F32 = jnp.float32
BF16 = jnp.bfloat16


def mm(a, b):
    return jnp.dot(a, b, preferred_element_type=F32)


def mm_nt(a, b):
    return lax.dot_general(a, b, (((1,), (1,)), ((), ())), preferred_element_type=F32)


def mm_tn(a, b):
    return lax.dot_general(a, b, (((0,), (0,)), ((), ())), preferred_element_type=F32)


def split(x):
    high = x.astype(BF16)
    return high, (x - high.astype(F32)).astype(BF16)


def token_gradients(weights, keys, values):
    w_one, w_three, w_two_t = weights
    gate = mm(keys, w_one)
    up = mm(keys, w_three)
    d_hidden = -mm(values, w_two_t)
    sig = jax.nn.sigmoid(gate)
    silu = gate * sig
    d_gate = d_hidden * up * sig * (1.0 + gate * (1.0 - sig))
    d_up = d_hidden * silu
    hidden = silu * up
    return (
        mm_tn(keys, d_gate.astype(BF16)),
        mm_tn(keys, d_up.astype(BF16)),
        -mm_tn(values, hidden.astype(BF16)),
    )


def orthogonalize(mats):
    a, b, c = SCHULZ_COEFFS
    centre = -b / (2.0 * c)
    rest = a - b * b / (4.0 * c)
    rows = mats[0].shape[0]
    shape = (rows, rows)
    diag = lax.broadcasted_iota(jnp.int32, shape, 0) == lax.broadcasted_iota(jnp.int32, shape, 1)
    xs = [m * (1.0 / (jnp.sqrt(jnp.sum(m * m)) + EPSILON)) for m in mats]
    for sweep in range(NS_STEPS):
        if sweep < 2:
            lows = [x.astype(BF16) for x in xs]
            grams = [mm_nt(x, x) for x in lows]
            halves = [g.astype(BF16) for g in grams]
            polys = [(b * g + c * mm(h, h)).astype(BF16) for g, h in zip(grams, halves)]
            xs = [a * x + mm(p, low) for x, p, low in zip(xs, polys, lows)]
        elif sweep == 2:
            pairs = [split(x) for x in xs]
            grams = [mm_nt(h, h) + mm_nt(h, l) + mm_nt(l, h) for h, l in pairs]
            gpairs = [split(g) for g in grams]
            polys = [
                b * g + c * (mm(h, h) + mm(h, l) + mm(l, h)) for g, (h, l) in zip(grams, gpairs)
            ]
            ppairs = [split(p) for p in polys]
            xs = [
                a * x + (mm(ph, h) + mm(ph, l) + mm(pl_, h))
                for x, (ph, pl_), (h, l) in zip(xs, ppairs, pairs)
            ]
        else:
            lows = [x.astype(BF16) for x in xs]
            grams = [mm_nt(x, x) for x in lows]
            moved = [jnp.where(diag, g - centre, g).astype(BF16) for g in grams]
            polys = [(c * mm(h, h)).astype(BF16) for h in moved]
            xs = [rest * x + mm(p, low) for x, p, low in zip(xs, polys, lows)]
    return xs


def normed_forward(weights, queries):
    w_one, w_three, w_two_t = [split(w) for w in weights]
    gate = mm(queries, w_one[0]) + mm(queries, w_one[1])
    up = mm(queries, w_three[0]) + mm(queries, w_three[1])
    hidden = (gate * jax.nn.sigmoid(gate) * up).astype(BF16)
    out = mm_nt(hidden, w_two_t[0]) + mm_nt(hidden, w_two_t[1])
    return out * lax.rsqrt(jnp.mean(out * out, axis=-1, keepdims=True) + EPSILON)


def window_attention(queries, own, behind, has_behind):
    tok, width = queries.shape
    head_dim = width
    scale = 1.0 / math.sqrt(head_dim)
    shape = (tok, tok)
    row = lax.broadcasted_iota(jnp.int32, shape, 0)
    col = lax.broadcasted_iota(jnp.int32, shape, 1)
    allow_own = (row >= col) & (row - col < WINDOW)
    allow_behind = (row + tok - col < WINDOW) & has_behind
    s_own = jnp.where(allow_own, mm_nt(queries, own[:, :width]) * scale, -1e30)
    s_behind = jnp.where(allow_behind, mm_nt(queries, behind[:, :width]) * scale, -1e30)
    top = jnp.maximum(
        jnp.max(s_own, axis=1, keepdims=True), jnp.max(s_behind, axis=1, keepdims=True)
    )
    e_own = jnp.where(allow_own, jnp.exp(s_own - top), 0.0)
    e_behind = jnp.where(allow_behind, jnp.exp(s_behind - top), 0.0)
    total = jnp.sum(e_own, axis=1, keepdims=True) + jnp.sum(e_behind, axis=1, keepdims=True)
    inv = 1.0 / total
    return mm((e_own * inv).astype(BF16), own[:, width:]) + mm(
        (e_behind * inv).astype(BF16), behind[:, width:]
    )


def call(kernel, outs, args, flops=0, scratch=()):
    vmem = pl.BlockSpec(memory_space=pltpu.VMEM)
    size = sum(math.prod(a.shape) * a.dtype.itemsize for a in list(args) + list(outs))
    return pl.pallas_call(
        kernel,
        out_shape=tuple(jax.ShapeDtypeStruct(o.shape, o.dtype) for o in outs),
        in_specs=[vmem] * len(args),
        out_specs=tuple([vmem] * len(outs)),
        scratch_shapes=list(scratch),
        compiler_params=pltpu.CompilerParams(vmem_limit_bytes=VMEM_BYTES),
        cost_estimate=pl.CostEstimate(flops=flops, bytes_accessed=size, transcendentals=0),
    )(*args)


def like(shape, dtype):
    return jax.ShapeDtypeStruct(shape, dtype)


def gradients(weights, runs, before):
    rows, hidden = weights[0].shape
    count = len(runs)

    def kernel(*refs):
        w = [r[...].astype(BF16) for r in refs[:3]]
        run_refs = refs[3 : 3 + count]
        prev = refs[3 + count : -3]
        sums = [p[...] for p in prev] if prev else None
        for run in run_refs:
            new = token_gradients(w, run[:, :rows], run[:, rows:])
            sums = list(new) if sums is None else [s + n for s, n in zip(sums, new)]
        for out, value in zip(refs[-3:], sums):
            out[...] = value

    tokens = sum(r.shape[0] for r in runs)
    args = list(weights) + list(runs) + (list(before) if before is not None else [])
    outs = [like((rows, hidden), F32)] * 3
    return call(kernel, outs, args, flops=12 * tokens * rows * hidden)


def update(weights, grads, last_runs, queries=None, block=None):
    rows, hidden = weights[0].shape
    count = len(last_runs)
    mixes = queries is not None

    def kernel(*refs):
        w = [r[...] for r in refs[:3]]
        sums = [r[...] for r in refs[3:6]]
        run_refs = refs[6 : 6 + count]
        low = [x.astype(BF16) for x in w]
        for run in run_refs:
            new = token_gradients(low, run[:, :rows], run[:, rows:])
            sums = [s + n for s, n in zip(sums, new)]
        ortho = orthogonalize(sums)
        fresh = [x - LEARN_RATE * o for x, o in zip(w, ortho)]
        if mixes:
            q_ref = refs[6 + count]
            outs = refs[7 + count :]
            for out, value in zip(outs, fresh):
                out[...] = value
            outs[3][...] = normed_forward(fresh, q_ref[block])
        else:
            outs = refs[6 + count :]
            outs[0][0] = fresh[0]
            outs[1][0] = fresh[1]
            outs[2][0] = fresh[2].T

    args = list(weights) + list(grads) + list(last_runs)
    if mixes:
        args += [queries]
        outs = [like((rows, hidden), F32)] * 3 + [like(queries.shape[1:], F32)]
    else:
        outs = [like((1, rows, hidden), F32)] * 2 + [like((1, hidden, rows), F32)]
    flops = 3 * 5 * 2 * (2 * rows * rows * hidden + rows**3) * 2
    return call(kernel, outs, args, flops=flops)


def later_mix(queries, own, behind, normed, block):
    def kernel(q_ref, own_ref, behind_ref, normed_ref, out_ref):
        has_behind = (lax.axis_index("seq") > 0) | (block > 0)
        att = window_attention(q_ref[block], own_ref[...], behind_ref[...], has_behind)
        out_ref[...] = (att + normed_ref[...]).astype(BF16)

    tok, width = queries.shape[1:]
    return call(
        kernel,
        [like((tok, width), BF16)],
        [queries, own, behind, normed],
        flops=8 * tok * tok * width,
    )[0]


def first_mix(queries, own, others, tables, weights):
    count = len(others)

    def kernel(q_ref, own_ref, *refs):
        other_refs = refs[:count]
        one_ref, three_ref, two_ref, out_ref, behind_ref = refs[count:]
        me = lax.axis_index("seq")
        behind_ref[...] = own_ref[...]
        for ref, (table, first_row) in zip(other_refs, tables):
            owner = sum(jnp.where(me == d, o, 0) for d, o in enumerate(table))

            @pl.when(owner == me - 1)
            def _():
                behind_ref[first_row : first_row + ref.shape[0], :] = ref[...]

        queries = q_ref[0]
        att = window_attention(queries, own_ref[...], behind_ref[...], me > 0)
        w = [one_ref[...], three_ref[...], two_ref[...]]
        out_ref[...] = (att + normed_forward(w, queries)).astype(BF16)

    tok, width = queries.shape[1:]
    return call(
        kernel,
        [like((tok, width), BF16)],
        [queries, own] + list(others) + list(weights),
        flops=20 * tok * tok * width,
        scratch=[pltpu.VMEM(own.shape, BF16)],
    )[0]


def loss_tile(loss):
    high = loss.astype(BF16).astype(F32)
    row = lax.broadcasted_iota(jnp.int32, (LOSS_ROWS, LANES), 0)
    return jnp.where(row < LOSS_ROWS // 2, high, loss - high).astype(BF16)


def tile_loss(tile):
    return jnp.sum(tile.astype(F32)) * (1.0 / (LOSS_ROWS // 2 * LANES))


def project(mixed_parts, proj_parts, teacher, block, before, chunks):
    count = len(mixed_parts)
    tok, width = mixed_parts[0].shape
    cols = teacher.shape[2]
    extra = [] if before is None else list(before)
    chunk = cols // max(chunks, 1)

    def kernel(*refs):
        mixed_refs, proj_refs = refs[:count], refs[count : 2 * count]
        teacher_ref = refs[2 * count]
        before_refs = refs[2 * count + 1 : 2 * count + 1 + len(extra)]
        outs = refs[2 * count + 1 + len(extra) :]
        student_ref, term_ref, loss_ref = outs[:3]
        low_ref = outs[-2] if chunks else outs[-1]
        full_ref = outs[-1] if chunks else term_ref
        summed = mm(mixed_refs[0][...], proj_refs[0][...])
        for m, p in zip(mixed_refs[1:], proj_refs[1:]):
            summed = summed + mm(m[...], p[...])
        low_ref[...] = summed.astype(BF16)
        start = pl.multiple_of(lax.axis_index("head") * width, width)
        student_ref[...] = low_ref[:, pl.ds(start, width)]
        diff = summed - teacher_ref[block].astype(F32)
        term = mm_tn(mixed_refs[0][...], diff.astype(BF16))
        loss = jnp.sum(diff * diff)
        if before_refs:
            term = term + before_refs[0][...]
            loss = loss + jnp.max(before_refs[1][...])
        full_ref[...] = term
        loss_ref[...] = jnp.full((8, LANES), loss, F32)
        if chunks:
            place = lax.axis_index("seq")
            tile = loss_tile(loss)

            def part(index):
                return full_ref[:, pl.ds(pl.multiple_of(index * chunk, chunk), chunk)]

            term_ref[...] = part(place)
            for offset, send in enumerate(outs[3:-2], start=1):
                send[:width, :] = part(place ^ offset).astype(BF16)
                for at in range(0, chunk, LANES):
                    send[width:, at : at + LANES] = tile

    outs = [like((tok, width), BF16), like((width, chunk), F32), like((8, LANES), F32)]
    outs += [like((width + LOSS_ROWS, chunk), BF16)] * max(chunks - 1, 0)
    scratch = [pltpu.VMEM((tok, cols), BF16)]
    if chunks:
        scratch.append(pltpu.VMEM((width, cols), F32))
    return call(
        kernel,
        outs,
        list(mixed_parts) + list(proj_parts) + [teacher] + extra,
        flops=2 * tok * cols * width * (count + 1),
        scratch=scratch,
    )


def outer_total(own, loss, gots, grad_scale, loss_scale):
    width, chunk = own.shape

    def kernel(own_ref, loss_ref, *rest):
        got_refs, out_ref, new_loss_ref = rest[:-2], rest[-2], rest[-1]
        total = own_ref[...]
        sq = jnp.max(loss_ref[...])
        for got in got_refs:
            total = total + got[:width, :].astype(F32)
            sq = sq + tile_loss(got[width:, :LANES])
        out_ref[...] = (total * grad_scale).astype(BF16)
        new_loss_ref[...] = jnp.full((8, LANES), sq * loss_scale, F32)

    return call(
        kernel, [like((width, chunk), BF16), like((8, LANES), F32)], [own, loss] + list(gots)
    )


def assemble(pieces, offsets, cols):
    width, chunk = pieces[0].shape
    count = len(pieces)

    def kernel(*refs):
        out_ref = refs[-1]
        me = lax.axis_index("seq")
        for ref, offset in zip(refs[:count], offsets):
            start = pl.multiple_of((me ^ offset) * chunk, chunk)
            out_ref[:, pl.ds(start, chunk)] = ref[...].astype(F32)

    return call(kernel, [like((width, cols), F32)], list(pieces))[0]


def ring_order(size):
    return list(range(0, size, 2)) + list(range(size - 1 - size % 2, 0, -2))


class Ring:
    def __init__(self, block, axis):
        size = lax.axis_size(axis)
        self.block, self.axis, self.size = block, axis, size
        self.order = ring_order(size)
        self.ahead = [(self.order[i], self.order[(i + 1) % size]) for i in range(size)]
        self.back = [(b, a) for a, b in self.ahead]
        self.up = self.down = block
        self.done = 0
        self.got = []

    def source(self, distance):
        table = [0] * self.size
        for i, d in enumerate(self.order):
            table[d] = self.order[(i - distance) % self.size]
        return table

    def step(self, *earlier):
        self.done += 1
        up, down = after(self.up, *earlier), after(self.down, *earlier)
        if 2 * self.done == self.size:
            rows = self.block.shape[0] // 2
            one = lax.ppermute(up[:rows], self.axis, self.ahead)
            two = lax.ppermute(down[rows:], self.axis, self.back)
            self.got += [(one, self.source(self.done), 0), (two, self.source(self.done), rows)]
            return [one, two]
        self.up = lax.ppermute(up, self.axis, self.ahead)
        self.down = lax.ppermute(down, self.axis, self.back)
        self.got += [(self.up, self.source(self.done), 0), (self.down, self.source(-self.done), 0)]
        return [self.up, self.down]


def partner(block, axis, bit):
    size = lax.axis_size(axis)
    return lax.ppermute(block, axis, [(i ^ bit, i) for i in range(size)])


def cube_gather(block, axis):
    parts = [block]
    bit = lax.axis_size(axis) // 2
    while bit:
        parts += [partner(p, axis, bit) for p in parts]
        bit //= 2
    return parts


def from_behind(block, axis):
    size = lax.axis_size(axis)
    return lax.ppermute(block, axis, [((i - 1) % size, i) for i in range(size)])


def after(value, *earlier):
    return lax.optimization_barrier((value,) + earlier)[0]


def local(query_rows, key_rows, value_rows, first_fast, third_fast, second_fast, out_proj, teacher):
    block_count, tok, head_dim = query_rows.shape
    seq = lax.axis_size("seq")
    cols = out_proj.shape[1]
    total_rows = block_count * tok * seq
    pos = lax.axis_index("seq")
    gathers = seq <= 8 and seq % 2 == 0
    grad_scale = 1.0 / math.sqrt(total_rows)
    loss_scale = 1.0 / (total_rows * cols)
    weights = (first_fast[0], third_fast[0], second_fast[0].T)

    kv = [jnp.concatenate([key_rows[c], value_rows[c]], axis=1) for c in range(block_count)]
    rims = [kv[0]] + [jnp.where(pos == seq - 1, kv[c - 1], kv[c]) for c in range(1, block_count)]

    def ring_gradients(ring, weights, runs, *earlier):
        grads = None
        runs = [after(ring.block, *earlier)] + runs
        while 2 * ring.done < ring.size:
            later = ring.step(*(grads or ())[:1])
            grads = gradients(weights, runs, grads)
            runs = later
        return grads, runs

    mixed = []
    history = [weights]
    rings = []
    proj_parts = None
    if gathers:
        earlier = ()
        for c in range(block_count - 1):
            ring = Ring(after(kv[c], *earlier), "seq")
            rings.append(ring)
            runs = ring.step()
            if proj_parts is None:
                proj_parts = cube_gather(after(out_proj, runs[0]), "head")
            grads, final = ring_gradients(ring, weights, runs)
            earlier = (ring.up, ring.down)
            behind = from_behind(after(rims[c + 1], *earlier), "seq")
            if c + 2 == block_count:
                last_ring = Ring(after(kv[c + 1], *earlier), "seq")
                last_runs = last_ring.step()
            *fresh, normed = update(weights, grads, final, query_rows, c + 1)
            weights = tuple(fresh)
            history.append(weights)
            mixed.append(later_mix(query_rows, kv[c + 1], behind, normed, c + 1))
        others = [block for block, _, _ in rings[0].got]
        tables = [(table, row) for _, table, row in rings[0].got]
    else:
        proj_parts = cube_gather(out_proj, "head")
        for c in range(block_count - 1):
            grads = lax.psum(gradients(weights, [kv[c]], None), "seq")
            behind = from_behind(rims[c + 1], "seq")
            *fresh, normed = update(weights, grads, [], query_rows, c + 1)
            weights = tuple(fresh)
            history.append(weights)
            mixed.append(later_mix(query_rows, kv[c + 1], behind, normed, c + 1))
        others = [from_behind(rims[0], "seq")]
        tables = [([(d - 1) % seq for d in range(seq)], 0)]
    mixed.insert(0, first_mix(query_rows, after(kv[0], *mixed[-1:]), others, tables, history[0]))

    chunks = seq if gathers and seq & (seq - 1) == 0 and cols % (seq * LANES) == 0 else 0
    students = [None] * block_count
    before = None
    if gathers:
        mixed[-1] = after(mixed[-1], *last_runs)
    for c in range(block_count):
        last = c + 1 == block_count
        parts = cube_gather(mixed[c], "head")
        if last and gathers:
            grads = gradients(weights, [kv[c]] + last_runs, None)
            next_runs = last_ring.step()
            parts[-1] = after(parts[-1], *next_runs)
        students[c], *rest = project(
            parts, proj_parts, teacher, c, before, chunks if last else 0
        )
        before = rest
    term, loss, *sends = before

    if gathers:
        while 2 * last_ring.done < seq:
            runs, next_runs = next_runs, last_ring.step()
            grads = gradients(weights, runs, grads)
        final = next_runs
    else:
        grads, final = lax.psum(gradients(weights, [kv[-1]], None), "seq"), []
    new_first, new_third, new_second = update(weights, grads, final)

    if chunks:
        gots = [partner(s, "seq", m) for m, s in enumerate(sends, start=1)]
        term = after(term, *final)
        piece, loss = outer_total(term, loss, gots, grad_scale, loss_scale)
        line = [(2 * m, partner(piece, "seq", 2 * m)) for m in range(1, seq // 2)]
        pieces = [(0, piece)] + line
        pieces += [(m + 1, partner(p, "seq", 1)) for m, p in pieces]
        out_grad = assemble([p for _, p in pieces], [m for m, _ in pieces], cols)
        distill_loss = loss[0, 0]
    else:
        term, loss = lax.psum((term, loss), "seq")
        out_grad = term * grad_scale
        distill_loss = loss[0, 0] * loss_scale
    return (jnp.stack(students), out_grad, new_first, new_third, new_second, distill_loss)


def solution(mesh):
    in_specs = (
        P(None, "seq", "head"),
        P(None, "seq", "head"),
        P(None, "seq", "head"),
        P("head", None, None),
        P("head", None, None),
        P("head", None, None),
        P("head", None),
        P(None, "seq", None),
    )
    out_specs = (
        P(None, "seq", "head"),
        P("head", None),
        P("head", None, None),
        P("head", None, None),
        P("head", None, None),
        P(),
    )
    return jax.shard_map(local, mesh=mesh, in_specs=in_specs, out_specs=out_specs, check_vma=False)
```

```python
import functools
import math

import jax
import jax.numpy as jnp
from jax import lax
from jax.experimental import pallas as pl
from jax.experimental.pallas import tpu as pltpu
from jax.sharding import PartitionSpec as P

WINDOW = 256
NS_STEPS = 5
SCHULZ_COEFFS = (3.4445, -4.775, 2.0315)
LEARN_RATE = 0.5
EPSILON = 1e-06
LANES = 128
LOSS_ROWS = 16
VMEM_BYTES = 40 * 1024 * 1024

F32 = jnp.float32
BF16 = jnp.bfloat16


def mm(a, b):
    return jnp.dot(a, b, preferred_element_type=F32)


def mm_nt(a, b):
    return lax.dot_general(a, b, (((1,), (1,)), ((), ())), preferred_element_type=F32)


def mm_tn(a, b):
    return lax.dot_general(a, b, (((0,), (0,)), ((), ())), preferred_element_type=F32)


def split(x):
    high = x.astype(BF16)
    return high, (x - high.astype(F32)).astype(BF16)


def token_gradients(weights, keys, values):
    w_one, w_three, w_two_t = weights
    gate = mm(keys, w_one)
    up = mm(keys, w_three)
    d_hidden = -mm(values, w_two_t)
    sig = jax.nn.sigmoid(gate)
    silu = gate * sig
    d_gate = d_hidden * up * sig * (1.0 + gate * (1.0 - sig))
    d_up = d_hidden * silu
    hidden = silu * up
    return (
        mm_tn(keys, d_gate.astype(BF16)),
        mm_tn(keys, d_up.astype(BF16)),
        -mm_tn(values, hidden.astype(BF16)),
    )


def orthogonalize(mats):
    a, b, c = SCHULZ_COEFFS
    centre = -b / (2.0 * c)
    rest = a - b * b / (4.0 * c)
    rows = mats[0].shape[0]
    shape = (rows, rows)
    diag = lax.broadcasted_iota(jnp.int32, shape, 0) == lax.broadcasted_iota(jnp.int32, shape, 1)
    xs = [m * (1.0 / (jnp.sqrt(jnp.sum(m * m)) + EPSILON)) for m in mats]
    for sweep in range(NS_STEPS):
        if sweep < 2:
            lows = [x.astype(BF16) for x in xs]
            grams = [mm_nt(x, x) for x in lows]
            halves = [g.astype(BF16) for g in grams]
            polys = [(b * g + c * mm(h, h)).astype(BF16) for g, h in zip(grams, halves)]
            xs = [a * x + mm(p, low) for x, p, low in zip(xs, polys, lows)]
        else:
            lows = [x.astype(BF16) for x in xs]
            grams = [mm_nt(x, x) for x in lows]
            moved = [jnp.where(diag, g - centre, g) for g in grams]
            if sweep == 2:
                pairs = [split(m) for m in moved]
                polys = [split(c * (mm(h, h) + mm(h, l) + mm(l, h))) for h, l in pairs]
            else:
                halves = [m.astype(BF16) for m in moved]
                polys = [((c * mm(h, h)).astype(BF16),) for h in halves]
            xs = [rest * x + sum(mm(p, low) for p in poly) for x, poly, low in zip(xs, polys, lows)]
    return xs


def normed_forward(weights, queries):
    w_one, w_three, w_two_t = [split(w) for w in weights]
    gate = mm(queries, w_one[0]) + mm(queries, w_one[1])
    up = mm(queries, w_three[0]) + mm(queries, w_three[1])
    hidden = (gate * jax.nn.sigmoid(gate) * up).astype(BF16)
    out = mm_nt(hidden, w_two_t[0]) + mm_nt(hidden, w_two_t[1])
    return out * lax.rsqrt(jnp.mean(out * out, axis=-1, keepdims=True) + EPSILON)


def window_attention(queries, own, behind, has_behind):
    tok, width = queries.shape
    head_dim = width
    scale = 1.0 / math.sqrt(head_dim)
    shape = (tok, tok)
    row = lax.broadcasted_iota(jnp.int32, shape, 0)
    col = lax.broadcasted_iota(jnp.int32, shape, 1)
    allow_own = (row >= col) & (row - col < WINDOW)
    allow_behind = (row + tok - col < WINDOW) & has_behind
    s_own = jnp.where(allow_own, mm_nt(queries, own[:, :width]) * scale, -1e30)
    s_behind = jnp.where(allow_behind, mm_nt(queries, behind[:, :width]) * scale, -1e30)
    top = jnp.maximum(
        jnp.max(s_own, axis=1, keepdims=True), jnp.max(s_behind, axis=1, keepdims=True)
    )
    e_own = jnp.where(allow_own, jnp.exp(s_own - top), 0.0)
    e_behind = jnp.where(allow_behind, jnp.exp(s_behind - top), 0.0)
    total = jnp.sum(e_own, axis=1, keepdims=True) + jnp.sum(e_behind, axis=1, keepdims=True)
    inv = 1.0 / total
    return mm((e_own * inv).astype(BF16), own[:, width:]) + mm(
        (e_behind * inv).astype(BF16), behind[:, width:]
    )


def call(kernel, outs, args, flops=0, scratch=(), scalars=0):
    vmem = pl.BlockSpec(memory_space=pltpu.VMEM)
    smem = pl.BlockSpec(memory_space=pltpu.SMEM)
    size = sum(math.prod(a.shape) * a.dtype.itemsize for a in list(args) + list(outs))
    return pl.pallas_call(
        kernel,
        out_shape=tuple(jax.ShapeDtypeStruct(o.shape, o.dtype) for o in outs),
        in_specs=[vmem] * len(args),
        out_specs=tuple([vmem] * (len(outs) - scalars) + [smem] * scalars),
        scratch_shapes=list(scratch),
        compiler_params=pltpu.CompilerParams(vmem_limit_bytes=VMEM_BYTES),
        cost_estimate=pl.CostEstimate(flops=flops, bytes_accessed=size, transcendentals=0),
    )(*args)


def like(shape, dtype):
    return jax.ShapeDtypeStruct(shape, dtype)


def gradients(weights, runs, before):
    rows, hidden = weights[0].shape
    count = len(runs)

    def kernel(*refs):
        w = [r[...].astype(BF16) for r in refs[:3]]
        run_refs = refs[3 : 3 + count]
        prev = refs[3 + count : -3]
        sums = [p[...] for p in prev] if prev else None
        for run in run_refs:
            new = token_gradients(w, run[:, :rows], run[:, rows:])
            sums = list(new) if sums is None else [s + n for s, n in zip(sums, new)]
        for out, value in zip(refs[-3:], sums):
            out[...] = value

    tokens = sum(r.shape[0] for r in runs)
    args = list(weights) + list(runs) + (list(before) if before is not None else [])
    outs = [like((rows, hidden), F32)] * 3
    return call(kernel, outs, args, flops=12 * tokens * rows * hidden)


def update(weights, grads, last_runs, queries=None, block=None):
    rows, hidden = weights[0].shape
    count = len(last_runs)
    mixes = queries is not None

    def kernel(*refs):
        w = [r[...] for r in refs[:3]]
        sums = [r[...] for r in refs[3:6]]
        run_refs = refs[6 : 6 + count]
        low = [x.astype(BF16) for x in w]
        for run in run_refs:
            new = token_gradients(low, run[:, :rows], run[:, rows:])
            sums = [s + n for s, n in zip(sums, new)]
        ortho = orthogonalize(sums)
        fresh = [x - LEARN_RATE * o for x, o in zip(w, ortho)]
        if mixes:
            q_ref = refs[6 + count]
            outs = refs[7 + count :]
            for out, value in zip(outs, fresh):
                out[...] = value
            outs[3][...] = normed_forward(fresh, q_ref[block])
        else:
            outs = refs[6 + count :]
            outs[0][0] = fresh[0]
            outs[1][0] = fresh[1]
            outs[2][0] = fresh[2].T

    args = list(weights) + list(grads) + list(last_runs)
    if mixes:
        args += [queries]
        outs = [like((rows, hidden), F32)] * 3 + [like(queries.shape[1:], F32)]
    else:
        outs = [like((1, rows, hidden), F32)] * 2 + [like((1, hidden, rows), F32)]
    flops = 3 * 5 * 2 * (2 * rows * rows * hidden + rows**3) * 2
    return call(kernel, outs, args, flops=flops)


def later_mix(queries, own, behind, normed, block):
    def kernel(q_ref, own_ref, behind_ref, normed_ref, out_ref):
        has_behind = (lax.axis_index("seq") > 0) | (block > 0)
        att = window_attention(q_ref[block], own_ref[...], behind_ref[...], has_behind)
        out_ref[...] = (att + normed_ref[...]).astype(BF16)

    tok, width = queries.shape[1:]
    return call(
        kernel,
        [like((tok, width), BF16)],
        [queries, own, behind, normed],
        flops=8 * tok * tok * width,
    )[0]


def first_mix(queries, own, others, tables, weights):
    count = len(others)

    def kernel(q_ref, own_ref, *refs):
        other_refs = refs[:count]
        one_ref, three_ref, two_ref, out_ref, behind_ref = refs[count:]
        me = lax.axis_index("seq")
        behind_ref[...] = own_ref[...]
        for ref, (table, first_row) in zip(other_refs, tables):
            owner = sum(jnp.where(me == d, o, 0) for d, o in enumerate(table))

            @pl.when(owner == me - 1)
            def _():
                behind_ref[first_row : first_row + ref.shape[0], :] = ref[...]

        queries = q_ref[0]
        att = window_attention(queries, own_ref[...], behind_ref[...], me > 0)
        w = [one_ref[...], three_ref[...], two_ref[...]]
        out_ref[...] = (att + normed_forward(w, queries)).astype(BF16)

    tok, width = queries.shape[1:]
    return call(
        kernel,
        [like((tok, width), BF16)],
        [queries, own] + list(others) + list(weights),
        flops=20 * tok * tok * width,
        scratch=[pltpu.VMEM(own.shape, BF16)],
    )[0]


def loss_tile(loss):
    high = loss.astype(BF16).astype(F32)
    row = lax.broadcasted_iota(jnp.int32, (LOSS_ROWS, LANES), 0)
    return jnp.where(row < LOSS_ROWS // 2, high, loss - high).astype(BF16)


def tile_loss(tile):
    return jnp.sum(tile.astype(F32)) * (1.0 / (LOSS_ROWS // 2 * LANES))


def project(mixed_parts, proj_parts, teacher, block, before, chunks):
    count = len(mixed_parts)
    tok, width = mixed_parts[0].shape
    cols = teacher.shape[2]
    extra = [] if before is None else list(before)
    chunk = cols // max(chunks, 1)

    def kernel(*refs):
        mixed_refs, proj_refs = refs[:count], refs[count : 2 * count]
        teacher_ref = refs[2 * count]
        before_refs = refs[2 * count + 1 : 2 * count + 1 + len(extra)]
        outs = refs[2 * count + 1 + len(extra) :]
        student_ref, term_ref, loss_ref = outs[:3]
        low_ref = outs[-2] if chunks else outs[-1]
        full_ref = outs[-1] if chunks else term_ref
        summed = mm(mixed_refs[0][...], proj_refs[0][...])
        for m, p in zip(mixed_refs[1:], proj_refs[1:]):
            summed = summed + mm(m[...], p[...])
        low_ref[...] = summed.astype(BF16)
        start = pl.multiple_of(lax.axis_index("head") * width, width)
        student_ref[...] = low_ref[:, pl.ds(start, width)]
        diff = summed - teacher_ref[block].astype(F32)
        term = mm_tn(mixed_refs[0][...], diff.astype(BF16))
        loss = jnp.sum(diff * diff)
        if before_refs:
            term = term + before_refs[0][...]
            loss = loss + jnp.max(before_refs[1][...])
        full_ref[...] = term
        loss_ref[...] = jnp.full((8, LANES), loss, F32)
        if chunks:
            place = lax.axis_index("seq")
            tile = loss_tile(loss)

            def part(index):
                return full_ref[:, pl.ds(pl.multiple_of(index * chunk, chunk), chunk)]

            term_ref[...] = part(place)
            for offset, send in enumerate(outs[3:-2], start=1):
                send[:width, :] = part(lax.rem(place + offset, chunks)).astype(BF16)
                for at in range(0, chunk, LANES):
                    send[width:, at : at + LANES] = tile

    outs = [like((tok, width), BF16), like((width, chunk), F32), like((8, LANES), F32)]
    outs += [like((width + LOSS_ROWS, chunk), BF16)] * max(chunks - 1, 0)
    scratch = [pltpu.VMEM((tok, cols), BF16)]
    if chunks:
        scratch.append(pltpu.VMEM((width, cols), F32))
    return call(
        kernel,
        outs,
        list(mixed_parts) + list(proj_parts) + [teacher] + extra,
        flops=2 * tok * cols * width * (count + 1),
        scratch=scratch,
    )


def outer_total(own, loss, gots, grad_scale, loss_scale):
    width, chunk = own.shape
    seq = len(gots) + 1

    def kernel(own_ref, loss_ref, *rest):
        got_refs, out_ref, new_loss_ref = rest[:-2], rest[-2], rest[-1]
        me = lax.axis_index("seq")
        total = own_ref[...]
        lane = lax.broadcasted_iota(jnp.int32, (LOSS_ROWS, LANES), 1)
        own_tile = loss_tile(jnp.max(loss_ref[...]))
        spread = jnp.where(lane == me, own_tile.astype(F32), 0.0)
        for offset, got in enumerate(got_refs, start=1):
            total = total + got[:width, :].astype(F32)
            here = lane == lax.rem(me + seq - offset, seq)
            spread = spread + jnp.where(here, got[width:, :LANES].astype(F32), 0.0)
        loss = jnp.sum(spread) * (2.0 / LOSS_ROWS)
        out_ref[...] = (total * grad_scale).astype(BF16)
        new_loss_ref[0, 0] = loss * loss_scale

    return call(
        kernel,
        [like((width, chunk), BF16), like((1, 1), F32)],
        [own, loss] + list(gots),
        scalars=1,
    )


def assemble(pieces, offsets, cols):
    width, chunk = pieces[0].shape
    count = len(pieces)

    def kernel(*refs):
        out_ref = refs[-1]
        me = lax.axis_index("seq")
        for ref, offset in zip(refs[:count], offsets):
            start = pl.multiple_of((me ^ offset) * chunk, chunk)
            out_ref[:, pl.ds(start, chunk)] = ref[...].astype(F32)

    return call(kernel, [like((width, cols), F32)], list(pieces))[0]


def ring_order(size):
    return list(range(0, size, 2)) + list(range(size - 1 - size % 2, 0, -2))


class Ring:
    def __init__(self, block, axis):
        size = lax.axis_size(axis)
        self.block, self.axis, self.size = block, axis, size
        self.order = ring_order(size)
        self.ahead = [(self.order[i], self.order[(i + 1) % size]) for i in range(size)]
        self.back = [(b, a) for a, b in self.ahead]
        self.up = self.down = block
        self.done = 0
        self.got = []

    def source(self, distance):
        table = [0] * self.size
        for i, d in enumerate(self.order):
            table[d] = self.order[(i - distance) % self.size]
        return table

    def step(self, *earlier):
        self.done += 1
        up, down = after(self.up, *earlier), after(self.down, *earlier)
        if 2 * self.done == self.size:
            rows = self.block.shape[0] // 2
            one = lax.ppermute(up[:rows], self.axis, self.ahead)
            two = lax.ppermute(down[rows:], self.axis, self.back)
            self.got += [(one, self.source(self.done), 0), (two, self.source(self.done), rows)]
            return [one, two]
        self.up = lax.ppermute(up, self.axis, self.ahead)
        self.down = lax.ppermute(down, self.axis, self.back)
        self.got += [(self.up, self.source(self.done), 0), (self.down, self.source(-self.done), 0)]
        return [self.up, self.down]


def partner(block, axis, bit):
    size = lax.axis_size(axis)
    return lax.ppermute(block, axis, [(i ^ bit, i) for i in range(size)])


def shifted(blocks, axis):
    size = lax.axis_size(axis)
    got = [None] * len(blocks)
    for far in range(size // 2, 0, -1):
        for shift in dict.fromkeys((far, size - far)):
            pairs = [(d, (d + shift) % size) for d in range(size)]
            got[shift - 1] = lax.ppermute(blocks[shift - 1], axis, pairs)
    return got


def cube_gather(block, axis):
    parts = [block]
    bit = lax.axis_size(axis) // 2
    while bit:
        parts += [partner(p, axis, bit) for p in parts]
        bit //= 2
    return parts


def from_behind(block, axis):
    size = lax.axis_size(axis)
    return lax.ppermute(block, axis, [((i - 1) % size, i) for i in range(size)])


def after(value, *earlier):
    return lax.optimization_barrier((value,) + earlier)[0]


def local(query_rows, key_rows, value_rows, first_fast, third_fast, second_fast, out_proj, teacher):
    block_count, tok, head_dim = query_rows.shape
    seq = lax.axis_size("seq")
    cols = out_proj.shape[1]
    total_rows = block_count * tok * seq
    pos = lax.axis_index("seq")
    gathers = seq <= 8 and seq % 2 == 0
    grad_scale = 1.0 / math.sqrt(total_rows)
    loss_scale = 1.0 / (total_rows * cols)
    weights = (first_fast[0], third_fast[0], second_fast[0].T)

    kv = [jnp.concatenate([key_rows[c], value_rows[c]], axis=1) for c in range(block_count)]
    rims = [kv[0]] + [jnp.where(pos == seq - 1, kv[c - 1], kv[c]) for c in range(1, block_count)]

    def ring_gradients(ring, weights, runs, *earlier):
        grads = None
        runs = [after(ring.block, *earlier)] + runs
        while 2 * ring.done < ring.size:
            later = ring.step(*(grads or ())[:1])
            grads = gradients(weights, runs, grads)
            runs = later
        return grads, runs

    mixed = []
    history = [weights]
    rings = []
    proj_parts = None
    if gathers:
        earlier = ()
        for c in range(block_count - 1):
            ring = Ring(after(kv[c], *earlier), "seq")
            rings.append(ring)
            runs = ring.step()
            if proj_parts is None:
                proj_parts = cube_gather(after(out_proj, runs[0]), "head")
            grads, final = ring_gradients(ring, weights, runs)
            earlier = (ring.up, ring.down)
            behind = from_behind(after(rims[c + 1], *earlier), "seq")
            if c + 2 == block_count:
                last_ring = Ring(after(kv[c + 1], *earlier), "seq")
                last_runs = last_ring.step()
            *fresh, normed = update(weights, grads, final, query_rows, c + 1)
            weights = tuple(fresh)
            history.append(weights)
            mixed.append(later_mix(query_rows, kv[c + 1], behind, normed, c + 1))
        others = [block for block, _, _ in rings[0].got]
        tables = [(table, row) for _, table, row in rings[0].got]
    else:
        proj_parts = cube_gather(out_proj, "head")
        for c in range(block_count - 1):
            grads = lax.psum(gradients(weights, [kv[c]], None), "seq")
            behind = from_behind(rims[c + 1], "seq")
            *fresh, normed = update(weights, grads, [], query_rows, c + 1)
            weights = tuple(fresh)
            history.append(weights)
            mixed.append(later_mix(query_rows, kv[c + 1], behind, normed, c + 1))
        others = [from_behind(rims[0], "seq")]
        tables = [([(d - 1) % seq for d in range(seq)], 0)]
    mixed.insert(0, first_mix(query_rows, after(kv[0], *mixed[-1:]), others, tables, history[0]))

    chunks = seq if gathers and seq & (seq - 1) == 0 and cols % (seq * LANES) == 0 else 0
    students = [None] * block_count
    before = None
    if gathers:
        mixed[-1] = after(mixed[-1], *last_runs)
    for c in range(block_count):
        last = c + 1 == block_count
        parts = cube_gather(mixed[c], "head")
        if last and gathers:
            grads = gradients(weights, [kv[c]] + last_runs, None)
            next_runs = last_ring.step()
            parts[-1] = after(parts[-1], *next_runs)
        students[c], *rest = project(
            parts, proj_parts, teacher, c, before, chunks if last else 0
        )
        before = rest
    term, loss, *sends = before

    if gathers:
        while 2 * last_ring.done < seq:
            runs, next_runs = next_runs, last_ring.step()
            grads = gradients(weights, runs, grads)
        final = next_runs
    else:
        grads, final = lax.psum(gradients(weights, [kv[-1]], None), "seq"), []
    new_first, new_third, new_second = update(weights, grads, final)

    if chunks:
        gots = shifted(sends, "seq")
        term = after(term, *final)
        piece, loss = outer_total(term, loss, gots, grad_scale, loss_scale)
        line = [(2 * m, partner(piece, "seq", 2 * m)) for m in range(1, seq // 2)]
        pieces = [(0, piece)] + line
        pieces += [(m + 1, partner(p, "seq", 1)) for m, p in pieces]
        out_grad = assemble([p for _, p in pieces], [m for m, _ in pieces], cols)
        distill_loss = loss.reshape(())
    else:
        term, loss = lax.psum((term, loss), "seq")
        out_grad = term * grad_scale
        distill_loss = loss[0, 0] * loss_scale
    return (jnp.stack(students), out_grad, new_first, new_third, new_second, distill_loss)


def solution(mesh):
    in_specs = (
        P(None, "seq", "head"),
        P(None, "seq", "head"),
        P(None, "seq", "head"),
        P("head", None, None),
        P("head", None, None),
        P("head", None, None),
        P("head", None),
        P(None, "seq", None),
    )
    out_specs = (
        P(None, "seq", "head"),
        P("head", None),
        P("head", None, None),
        P("head", None, None),
        P("head", None, None),
        P(),
    )
    return jax.shard_map(local, mesh=mesh, in_specs=in_specs, out_specs=out_specs, check_vma=False)
```

```python
import functools
import math

import jax
import jax.numpy as jnp
from jax import lax
from jax.experimental import pallas as pl
from jax.experimental.pallas import tpu as pltpu
from jax.sharding import PartitionSpec as P

WINDOW = 256
NS_STEPS = 5
SCHULZ_COEFFS = (3.4445, -4.775, 2.0315)
LEARN_RATE = 0.5
EPSILON = 1e-06
LANES = 128
LOSS_ROWS = 16
VMEM_BYTES = 40 * 1024 * 1024

F32 = jnp.float32
BF16 = jnp.bfloat16


def mm(a, b):
    return jnp.dot(a, b, preferred_element_type=F32)


def mm_nt(a, b):
    return lax.dot_general(a, b, (((1,), (1,)), ((), ())), preferred_element_type=F32)


def mm_tn(a, b):
    return lax.dot_general(a, b, (((0,), (0,)), ((), ())), preferred_element_type=F32)


def split(x):
    high = x.astype(BF16)
    return high, (x - high.astype(F32)).astype(BF16)


def token_gradients(weights, keys, values):
    w_one, w_three, w_two_t = weights
    gate = mm(keys, w_one)
    up = mm(keys, w_three)
    d_hidden = -mm(values, w_two_t)
    sig = jax.nn.sigmoid(gate)
    silu = gate * sig
    d_gate = d_hidden * up * (sig + silu * (1.0 - sig))
    d_up = d_hidden * silu
    hidden = silu * up
    both = mm_tn(keys, jnp.concatenate([d_gate.astype(BF16), d_up.astype(BF16)], axis=1))
    width = d_gate.shape[1]
    return (both[:, :width], both[:, width:], -mm_tn(values, hidden.astype(BF16)))


def orthogonalize(mats):
    a, b, c = SCHULZ_COEFFS
    centre = -b / (2.0 * c)
    rest = a - b * b / (4.0 * c)
    rows = mats[0].shape[0]
    shape = (rows, rows)
    diag = lax.broadcasted_iota(jnp.int32, shape, 0) == lax.broadcasted_iota(jnp.int32, shape, 1)
    xs = [m * (1.0 / (jnp.sqrt(jnp.sum(m * m)) + EPSILON)) for m in mats]
    for sweep in range(NS_STEPS):
        if sweep < 2:
            lows = [x.astype(BF16) for x in xs]
            grams = [mm_nt(x, x) for x in lows]
            halves = [g.astype(BF16) for g in grams]
            polys = [(b * g + c * mm(h, h)).astype(BF16) for g, h in zip(grams, halves)]
            xs = [a * x + mm(p, low) for x, p, low in zip(xs, polys, lows)]
        else:
            lows = [x.astype(BF16) for x in xs]
            grams = [mm_nt(x, x) for x in lows]
            moved = [jnp.where(diag, g - centre, g) for g in grams]
            if sweep == 2:
                pairs = [split(m) for m in moved]
                polys = [split(c * (mm(h, h) + mm(h, l) + mm(l, h))) for h, l in pairs]
            else:
                halves = [m.astype(BF16) for m in moved]
                polys = [((c * mm(h, h)).astype(BF16),) for h in halves]
            xs = [rest * x + sum(mm(p, low) for p in poly) for x, poly, low in zip(xs, polys, lows)]
    return xs


def normed_forward(weights, queries):
    w_one, w_three, w_two_t = [split(w) for w in weights]
    gate = mm(queries, w_one[0]) + mm(queries, w_one[1])
    up = mm(queries, w_three[0]) + mm(queries, w_three[1])
    hidden = (gate * jax.nn.sigmoid(gate) * up).astype(BF16)
    out = mm_nt(hidden, w_two_t[0]) + mm_nt(hidden, w_two_t[1])
    return out * lax.rsqrt(jnp.mean(out * out, axis=-1, keepdims=True) + EPSILON)


def window_attention(queries, own, behind, has_behind):
    tok, width = queries.shape
    head_dim = width
    scale = 1.0 / math.sqrt(head_dim)
    shape = (tok, tok)
    row = lax.broadcasted_iota(jnp.int32, shape, 0)
    col = lax.broadcasted_iota(jnp.int32, shape, 1)
    allow_own = (row >= col) & (row - col < WINDOW)
    allow_behind = (row + tok - col < WINDOW) & has_behind
    s_own = jnp.where(allow_own, mm_nt(queries, own[:, :width]) * scale, -1e30)
    s_behind = jnp.where(allow_behind, mm_nt(queries, behind[:, :width]) * scale, -1e30)
    top = jnp.maximum(
        jnp.max(s_own, axis=1, keepdims=True), jnp.max(s_behind, axis=1, keepdims=True)
    )
    e_own = jnp.where(allow_own, jnp.exp(s_own - top), 0.0)
    e_behind = jnp.where(allow_behind, jnp.exp(s_behind - top), 0.0)
    total = jnp.sum(e_own, axis=1, keepdims=True) + jnp.sum(e_behind, axis=1, keepdims=True)
    inv = 1.0 / total
    return mm((e_own * inv).astype(BF16), own[:, width:]) + mm(
        (e_behind * inv).astype(BF16), behind[:, width:]
    )


def call(kernel, outs, args, flops=0, scratch=(), scalars=0):
    vmem = pl.BlockSpec(memory_space=pltpu.VMEM)
    smem = pl.BlockSpec(memory_space=pltpu.SMEM)
    size = sum(math.prod(a.shape) * a.dtype.itemsize for a in list(args) + list(outs))
    return pl.pallas_call(
        kernel,
        out_shape=tuple(jax.ShapeDtypeStruct(o.shape, o.dtype) for o in outs),
        in_specs=[vmem] * len(args),
        out_specs=tuple([vmem] * (len(outs) - scalars) + [smem] * scalars),
        scratch_shapes=list(scratch),
        compiler_params=pltpu.CompilerParams(vmem_limit_bytes=VMEM_BYTES),
        cost_estimate=pl.CostEstimate(flops=flops, bytes_accessed=size, transcendentals=0),
    )(*args)


def like(shape, dtype):
    return jax.ShapeDtypeStruct(shape, dtype)


def gradients(weights, runs, before):
    rows, hidden = weights[0].shape
    count = len(runs)

    def kernel(*refs):
        w = [r[...].astype(BF16) for r in refs[:3]]
        run_refs = refs[3 : 3 + count]
        prev = refs[3 + count : -3]
        sums = [p[...] for p in prev] if prev else None
        for run in run_refs:
            new = token_gradients(w, run[:, :rows], run[:, rows:])
            sums = list(new) if sums is None else [s + n for s, n in zip(sums, new)]
        for out, value in zip(refs[-3:], sums):
            out[...] = value

    tokens = sum(r.shape[0] for r in runs)
    args = list(weights) + list(runs) + (list(before) if before is not None else [])
    outs = [like((rows, hidden), F32)] * 3
    return call(kernel, outs, args, flops=12 * tokens * rows * hidden)


def update(weights, grads, last_runs, queries=None, block=None):
    rows, hidden = weights[0].shape
    count = len(last_runs)
    mixes = queries is not None

    def kernel(*refs):
        w = [r[...] for r in refs[:3]]
        sums = [r[...] for r in refs[3:6]]
        run_refs = refs[6 : 6 + count]
        low = [x.astype(BF16) for x in w]
        for run in run_refs:
            new = token_gradients(low, run[:, :rows], run[:, rows:])
            sums = [s + n for s, n in zip(sums, new)]
        ortho = orthogonalize(sums)
        fresh = [x - LEARN_RATE * o for x, o in zip(w, ortho)]
        if mixes:
            q_ref = refs[6 + count]
            outs = refs[7 + count :]
            for out, value in zip(outs, fresh):
                out[...] = value
            outs[3][...] = normed_forward(fresh, q_ref[block])
        else:
            outs = refs[6 + count :]
            outs[0][0] = fresh[0]
            outs[1][0] = fresh[1]
            outs[2][0] = fresh[2].T

    args = list(weights) + list(grads) + list(last_runs)
    if mixes:
        args += [queries]
        outs = [like((rows, hidden), F32)] * 3 + [like(queries.shape[1:], F32)]
    else:
        outs = [like((1, rows, hidden), F32)] * 2 + [like((1, hidden, rows), F32)]
    flops = 3 * 5 * 2 * (2 * rows * rows * hidden + rows**3) * 2
    return call(kernel, outs, args, flops=flops)


def later_mix(queries, own, behind, normed, block):
    def kernel(q_ref, own_ref, behind_ref, normed_ref, out_ref):
        has_behind = (lax.axis_index("seq") > 0) | (block > 0)
        att = window_attention(q_ref[block], own_ref[...], behind_ref[...], has_behind)
        out_ref[...] = (att + normed_ref[...]).astype(BF16)

    tok, width = queries.shape[1:]
    return call(
        kernel,
        [like((tok, width), BF16)],
        [queries, own, behind, normed],
        flops=8 * tok * tok * width,
    )[0]


def first_mix(queries, own, others, tables, weights):
    count = len(others)

    def kernel(q_ref, own_ref, *refs):
        other_refs = refs[:count]
        one_ref, three_ref, two_ref, out_ref, behind_ref = refs[count:]
        me = lax.axis_index("seq")
        behind_ref[...] = own_ref[...]
        for ref, (table, first_row) in zip(other_refs, tables):
            owner = sum(jnp.where(me == d, o, 0) for d, o in enumerate(table))

            @pl.when(owner == me - 1)
            def _():
                behind_ref[first_row : first_row + ref.shape[0], :] = ref[...]

        queries = q_ref[0]
        att = window_attention(queries, own_ref[...], behind_ref[...], me > 0)
        w = [one_ref[...], three_ref[...], two_ref[...]]
        out_ref[...] = (att + normed_forward(w, queries)).astype(BF16)

    tok, width = queries.shape[1:]
    return call(
        kernel,
        [like((tok, width), BF16)],
        [queries, own] + list(others) + list(weights),
        flops=20 * tok * tok * width,
        scratch=[pltpu.VMEM(own.shape, BF16)],
    )[0]


def loss_tile(loss):
    high = loss.astype(BF16).astype(F32)
    row = lax.broadcasted_iota(jnp.int32, (LOSS_ROWS, LANES), 0)
    return jnp.where(row < LOSS_ROWS // 2, high, loss - high).astype(BF16)


def tile_loss(tile):
    return jnp.sum(tile.astype(F32)) * (1.0 / (LOSS_ROWS // 2 * LANES))


def project(mixed_parts, proj_parts, teacher, block, before, chunks):
    count = len(mixed_parts)
    tok, width = mixed_parts[0].shape
    cols = teacher.shape[2]
    extra = [] if before is None else list(before)
    chunk = cols // max(chunks, 1)

    def kernel(*refs):
        mixed_refs, proj_refs = refs[:count], refs[count : 2 * count]
        teacher_ref = refs[2 * count]
        before_refs = refs[2 * count + 1 : 2 * count + 1 + len(extra)]
        outs = refs[2 * count + 1 + len(extra) :]
        student_ref, term_ref, loss_ref = outs[:3]
        low_ref = outs[-2] if chunks else outs[-1]
        full_ref = outs[-1] if chunks else term_ref
        summed = mm(mixed_refs[0][...], proj_refs[0][...])
        for m, p in zip(mixed_refs[1:], proj_refs[1:]):
            summed = summed + mm(m[...], p[...])
        low_ref[...] = summed.astype(BF16)
        start = pl.multiple_of(lax.axis_index("head") * width, width)
        student_ref[...] = low_ref[:, pl.ds(start, width)]
        diff = summed - teacher_ref[block].astype(F32)
        term = mm_tn(mixed_refs[0][...], diff.astype(BF16))
        loss = jnp.sum(diff * diff)
        if before_refs:
            term = term + before_refs[0][...]
            loss = loss + jnp.max(before_refs[1][...])
        full_ref[...] = term
        loss_ref[...] = jnp.full((8, LANES), loss, F32)
        if chunks:
            place = lax.axis_index("seq")
            tile = loss_tile(loss)

            def part(index):
                return full_ref[:, pl.ds(pl.multiple_of(index * chunk, chunk), chunk)]

            term_ref[...] = part(place)
            for offset, send in enumerate(outs[3:-2], start=1):
                send[:width, :] = part(lax.rem(place + offset, chunks)).astype(BF16)
                for at in range(0, chunk, LANES):
                    send[width:, at : at + LANES] = tile

    outs = [like((tok, width), BF16), like((width, chunk), F32), like((8, LANES), F32)]
    outs += [like((width + LOSS_ROWS, chunk), BF16)] * max(chunks - 1, 0)
    scratch = [pltpu.VMEM((tok, cols), BF16)]
    if chunks:
        scratch.append(pltpu.VMEM((width, cols), F32))
    return call(
        kernel,
        outs,
        list(mixed_parts) + list(proj_parts) + [teacher] + extra,
        flops=2 * tok * cols * width * (count + 1),
        scratch=scratch,
    )


def outer_total(own, loss, gots, grad_scale, loss_scale):
    width, chunk = own.shape
    seq = len(gots) + 1

    def kernel(own_ref, loss_ref, *rest):
        got_refs, out_ref, new_loss_ref = rest[:-2], rest[-2], rest[-1]
        me = lax.axis_index("seq")
        total = own_ref[...]
        lane = lax.broadcasted_iota(jnp.int32, (LOSS_ROWS, LANES), 1)
        own_tile = loss_tile(jnp.max(loss_ref[...]))
        spread = jnp.where(lane == me, own_tile.astype(F32), 0.0)
        for offset, got in enumerate(got_refs, start=1):
            total = total + got[:width, :].astype(F32)
            here = lane == lax.rem(me + seq - offset, seq)
            spread = spread + jnp.where(here, got[width:, :LANES].astype(F32), 0.0)
        loss = jnp.sum(spread) * (2.0 / LOSS_ROWS)
        out_ref[...] = (total * grad_scale).astype(BF16)
        new_loss_ref[0, 0] = loss * loss_scale

    return call(
        kernel,
        [like((width, chunk), BF16), like((1, 1), F32)],
        [own, loss] + list(gots),
        scalars=1,
    )


def assemble(pieces, offsets, cols):
    width, chunk = pieces[0].shape
    count = len(pieces)

    def kernel(*refs):
        out_ref = refs[-1]
        me = lax.axis_index("seq")
        for ref, offset in zip(refs[:count], offsets):
            start = pl.multiple_of((me ^ offset) * chunk, chunk)
            out_ref[:, pl.ds(start, chunk)] = ref[...].astype(F32)

    return call(kernel, [like((width, cols), F32)], list(pieces))[0]


def ring_order(size):
    return list(range(0, size, 2)) + list(range(size - 1 - size % 2, 0, -2))


class Ring:
    def __init__(self, block, axis):
        size = lax.axis_size(axis)
        self.block, self.axis, self.size = block, axis, size
        self.order = ring_order(size)
        self.ahead = [(self.order[i], self.order[(i + 1) % size]) for i in range(size)]
        self.back = [(b, a) for a, b in self.ahead]
        self.up = self.down = block
        self.done = 0
        self.got = []

    def source(self, distance):
        table = [0] * self.size
        for i, d in enumerate(self.order):
            table[d] = self.order[(i - distance) % self.size]
        return table

    def step(self, *earlier):
        self.done += 1
        up, down = after(self.up, *earlier), after(self.down, *earlier)
        if 2 * self.done == self.size:
            rows = self.block.shape[0] // 2
            one = lax.ppermute(up[:rows], self.axis, self.ahead)
            two = lax.ppermute(down[rows:], self.axis, self.back)
            self.got += [(one, self.source(self.done), 0), (two, self.source(self.done), rows)]
            return [one, two]
        self.up = lax.ppermute(up, self.axis, self.ahead)
        self.down = lax.ppermute(down, self.axis, self.back)
        self.got += [(self.up, self.source(self.done), 0), (self.down, self.source(-self.done), 0)]
        return [self.up, self.down]


def partner(block, axis, bit):
    size = lax.axis_size(axis)
    return lax.ppermute(block, axis, [(i ^ bit, i) for i in range(size)])


def shifted(blocks, axis):
    size = lax.axis_size(axis)
    got = [None] * len(blocks)
    for far in range(size // 2, 0, -1):
        for shift in dict.fromkeys((far, size - far)):
            pairs = [(d, (d + shift) % size) for d in range(size)]
            got[shift - 1] = lax.ppermute(blocks[shift - 1], axis, pairs)
    return got


def cube_gather(block, axis):
    parts = [block]
    bit = lax.axis_size(axis) // 2
    while bit:
        parts += [partner(p, axis, bit) for p in parts]
        bit //= 2
    return parts


def from_behind(block, axis):
    size = lax.axis_size(axis)
    return lax.ppermute(block, axis, [((i - 1) % size, i) for i in range(size)])


def after(value, *earlier):
    return lax.optimization_barrier((value,) + earlier)[0]


def local(query_rows, key_rows, value_rows, first_fast, third_fast, second_fast, out_proj, teacher):
    block_count, tok, head_dim = query_rows.shape
    seq = lax.axis_size("seq")
    cols = out_proj.shape[1]
    total_rows = block_count * tok * seq
    pos = lax.axis_index("seq")
    gathers = seq <= 8 and seq % 2 == 0
    grad_scale = 1.0 / math.sqrt(total_rows)
    loss_scale = 1.0 / (total_rows * cols)
    weights = (first_fast[0], third_fast[0], second_fast[0].T)

    kv = [jnp.concatenate([key_rows[c], value_rows[c]], axis=1) for c in range(block_count)]
    rims = [kv[0]] + [jnp.where(pos == seq - 1, kv[c - 1], kv[c]) for c in range(1, block_count)]

    def ring_gradients(ring, weights, runs, *earlier):
        grads = None
        runs = [after(ring.block, *earlier)] + runs
        while 2 * ring.done < ring.size:
            later = ring.step(*(grads or ())[:1])
            grads = gradients(weights, runs, grads)
            runs = later
        return grads, runs

    mixed = []
    history = [weights]
    rings = []
    proj_parts = None
    if gathers:
        earlier = ()
        for c in range(block_count - 1):
            ring = Ring(after(kv[c], *earlier), "seq")
            rings.append(ring)
            runs = ring.step()
            if proj_parts is None:
                proj_parts = cube_gather(after(out_proj, runs[0]), "head")
            grads, final = ring_gradients(ring, weights, runs)
            earlier = (ring.up, ring.down)
            behind = from_behind(after(rims[c + 1], *earlier), "seq")
            if c + 2 == block_count:
                last_ring = Ring(after(kv[c + 1], *earlier), "seq")
                last_runs = last_ring.step()
            *fresh, normed = update(weights, grads, final, query_rows, c + 1)
            weights = tuple(fresh)
            history.append(weights)
            mixed.append(later_mix(query_rows, kv[c + 1], behind, normed, c + 1))
        others = [block for block, _, _ in rings[0].got]
        tables = [(table, row) for _, table, row in rings[0].got]
    else:
        proj_parts = cube_gather(out_proj, "head")
        for c in range(block_count - 1):
            grads = lax.psum(gradients(weights, [kv[c]], None), "seq")
            behind = from_behind(rims[c + 1], "seq")
            *fresh, normed = update(weights, grads, [], query_rows, c + 1)
            weights = tuple(fresh)
            history.append(weights)
            mixed.append(later_mix(query_rows, kv[c + 1], behind, normed, c + 1))
        others = [from_behind(rims[0], "seq")]
        tables = [([(d - 1) % seq for d in range(seq)], 0)]
    mixed.insert(0, first_mix(query_rows, after(kv[0], *mixed[-1:]), others, tables, history[0]))

    chunks = seq if gathers and seq & (seq - 1) == 0 and cols % (seq * LANES) == 0 else 0
    students = [None] * block_count
    before = None
    if gathers:
        mixed[-1] = after(mixed[-1], *last_runs)
    for c in range(block_count):
        last = c + 1 == block_count
        parts = cube_gather(mixed[c], "head")
        if last and gathers:
            grads = gradients(weights, [kv[c]] + last_runs, None)
            next_runs = last_ring.step()
            parts[-1] = after(parts[-1], *next_runs)
        students[c], *rest = project(
            parts, proj_parts, teacher, c, before, chunks if last else 0
        )
        before = rest
    term, loss, *sends = before

    if gathers:
        while 2 * last_ring.done < seq:
            runs, next_runs = next_runs, last_ring.step()
            grads = gradients(weights, runs, grads)
        final = next_runs
    else:
        grads, final = lax.psum(gradients(weights, [kv[-1]], None), "seq"), []
    new_first, new_third, new_second = update(weights, grads, final)

    if chunks:
        gots = shifted(sends, "seq")
        term = after(term, *final)
        piece, loss = outer_total(term, loss, gots, grad_scale, loss_scale)
        line = [(2 * m, partner(piece, "seq", 2 * m)) for m in range(1, seq // 2)]
        pieces = [(0, piece)] + line
        pieces += [(m + 1, partner(p, "seq", 1)) for m, p in pieces]
        out_grad = assemble([p for _, p in pieces], [m for m, _ in pieces], cols)
        distill_loss = loss.reshape(())
    else:
        term, loss = lax.psum((term, loss), "seq")
        out_grad = term * grad_scale
        distill_loss = loss[0, 0] * loss_scale
    return (jnp.stack(students), out_grad, new_first, new_third, new_second, distill_loss)


def solution(mesh):
    in_specs = (
        P(None, "seq", "head"),
        P(None, "seq", "head"),
        P(None, "seq", "head"),
        P("head", None, None),
        P("head", None, None),
        P("head", None, None),
        P("head", None),
        P(None, "seq", None),
    )
    out_specs = (
        P(None, "seq", "head"),
        P("head", None),
        P("head", None, None),
        P("head", None, None),
        P("head", None, None),
        P(),
    )
    return jax.shard_map(local, mesh=mesh, in_specs=in_specs, out_specs=out_specs, check_vma=False)
```
